512 devices in a mesh: row: 32 (over z_lo, y, core), col: 16 (over x, z_hi).
Axes of the slice: x: 4, y: 4, z: 16 (z_hi: 4, z_lo: 4; z = z_hi * 4 + z_lo), core: 2. Of those that a mesh axis runs over, the one named last changes fastest.
Arguments:
- tokens: bfloat16 [384, 6144], P('row', 'col'), may hold values from -6 to 6
- first_weight: bfloat16 [6144, 24576], P('col', 'row'), may hold values from -0.078125 to 0.078125
- first_tangent: bfloat16 [6144, 24576], P('col', 'row'), may hold values from -0.078125 to 0.078125
- second_weight: bfloat16 [24576, 6144], P('row', 'col'), may hold values from -0.0390625 to 0.0390625
- second_tangent: bfloat16 [24576, 6144], P('row', 'col'), may hold values from -0.0390625 to 0.0390625
Outputs:
- first_curvature: bfloat16 [6144, 24576], P('col', 'row')
- second_curvature: bfloat16 [24576, 6144], P('row', 'col')
The draws below stay inside these ranges and needn't reach their ends.
All inputs are finite; a program needn't handle non-finite values.
Results may differ from the reference program's by a relative error of at most 0.009.
Values may be sent and summed in bfloat16 or wider, within the bound.
No kernel may reach another device: no remote copies, remote signals or barrier semaphores. Data moves between devices by JAX's collectives and lax.ppermute only.
A program may use at most 64 MiB of HBM per device.

```python
import math
import jax
import jax.numpy as jnp
from jax import lax

D = 6144
F = 24576
TOKENS = 384


def steps_of(own_key, extent, pieces, low, largest):
    gain = 1.0
    for axis_at, blocks in pieces:
        steps = jax.random.uniform(jax.random.fold_in(jax.random.fold_in(own_key, 6), axis_at), (blocks,), jnp.float32, low / len(pieces), largest / len(pieces))
        gain = gain * jnp.repeat(jnp.exp(steps), extent[axis_at] // blocks).reshape((-1,) + (1,) * (len(extent) - 1 - axis_at))
    return gain


def noise(stream_key, extent, width, bound, shards=(), kind=jnp.bfloat16):
    array = jax.random.normal(stream_key, extent, jnp.float32) * width
    if len(shards) > 0:
        array = steps_of(stream_key, extent, shards, -0.22, 0.18) * array
    return jnp.clip(array, min=-bound, max=bound).astype(kind)


def setup_inputs(seed: int = 0) -> dict:
    splits = jax.random.split(jax.random.key(seed), 6)
    tokens = noise(splits[0], (TOKENS, D), 1.0, 6.0, ((0, 32), (1, 16)))
    first_weight = noise(splits[1], (D, F), D ** -0.5, 0.078125, ((0, 16), (1, 32)))
    first_tangent = noise(splits[2], (D, F), D ** -0.5, 0.078125, ((0, 16), (1, 32)))
    second_weight = noise(splits[3], (F, D), F ** -0.5, 0.0390625, ((0, 32), (1, 16)))
    second_tangent = noise(splits[4], (F, D), F ** -0.5, 0.0390625, ((0, 32), (1, 16)))
    return {"tokens": tokens, "first_weight": first_weight, "first_tangent": first_tangent, "second_weight": second_weight, "second_tangent": second_tangent}


sqrt_two_pi = 0.7978845608028654
cubic_coef = 0.044715

def gelu_parts(hidden_pre):
    inner_arg = sqrt_two_pi * (hidden_pre + cubic_coef * hidden_pre * hidden_pre * hidden_pre)
    hyper_tan = jnp.tanh(inner_arg)
    activation = 0.5 * hidden_pre * (1.0 + hyper_tan)
    derivative = 0.5 * (1.0 + hyper_tan) + 0.5 * hidden_pre * (1.0 - hyper_tan * hyper_tan) * sqrt_two_pi * (1.0 + 3.0 * cubic_coef * hidden_pre * hidden_pre)
    return (activation, derivative)

def reference(tokens, first_weight, first_tangent, second_weight, second_tangent):
    token_count = tokens.shape[0]
    hidden_pre = jnp.dot(tokens, first_weight, preferred_element_type=jnp.float32)
    tangent_pre = jnp.dot(tokens, first_tangent, preferred_element_type=jnp.float32)
    activation_full, derivative = gelu_parts(hidden_pre)
    activation = activation_full.astype(jnp.bfloat16)
    tangent_act = (derivative * tangent_pre).astype(jnp.bfloat16)
    out_sum = jnp.dot(tangent_act, second_weight, preferred_element_type=jnp.float32) + jnp.dot(activation, second_tangent, preferred_element_type=jnp.float32)
    tangent_out = out_sum.astype(jnp.bfloat16)
    grad_act = lax.dot_general(tangent_out, second_weight, (((1,), (1,)), ((), ())), preferred_element_type=jnp.float32)
    grad_pre = (grad_act * derivative).astype(jnp.bfloat16)
    scaling = 1.0 / math.sqrt(token_count)
    first_curvature = (lax.dot_general(tokens, grad_pre, (((0,), (0,)), ((), ())), preferred_element_type=jnp.float32) * scaling).astype(jnp.bfloat16)
    second_curvature = (lax.dot_general(activation, tangent_out, (((0,), (0,)), ((), ())), preferred_element_type=jnp.float32) * scaling).astype(jnp.bfloat16)
    return (first_curvature, second_curvature)
```

```python
import math

import jax
import jax.numpy as jnp
from jax import lax
from jax.sharding import Mesh, PartitionSpec as P

sqrt_two_pi = 0.7978845608028654
cubic_coef = 0.044715

ROW = ("z_lo", "y", "core")
f32, bf16 = jnp.float32, jnp.bfloat16


def dot(left_side, right_side, left_dim, right_dim):
    return lax.dot_general(
        left_side, right_side, (((left_dim,), (right_dim,)), ((), ())), preferred_element_type=f32
    )


def swap(blocks, axes):
    return lax.all_to_all(blocks, axes, 0, 0, tiled=True)


def scatter_sum(partial, axes, count):
    arrived = swap(partial.astype(bf16), axes)
    return jnp.sum(arrived.reshape(count, -1, arrived.shape[1]).astype(f32), axis=0)


def gather(block, axes, count):
    return swap(jnp.broadcast_to(block[None], (count,) + block.shape).reshape(-1, block.shape[1]), axes)


def scatter_sum_col(partial):
    return scatter_sum(scatter_sum(partial, "x", 4), "z_hi", 4)


def gather_col(block):
    return gather(gather(block, "z_hi", 4), "x", 4)


def activate(hidden_pre, tangent_pre):
    inner_arg = sqrt_two_pi * (hidden_pre + cubic_coef * hidden_pre * hidden_pre * hidden_pre)
    hyper_tan = jnp.tanh(inner_arg)
    activation = (0.5 * hidden_pre * (1.0 + hyper_tan)).astype(bf16)
    derivative = 0.5 * (1.0 + hyper_tan) + 0.5 * hidden_pre * (
        1.0 - hyper_tan * hyper_tan
    ) * sqrt_two_pi * (1.0 + 3.0 * cubic_coef * hidden_pre * hidden_pre)
    tangent_act = (derivative * tangent_pre).astype(bf16)
    return (activation, derivative, tangent_act)


def shards(tokens, first_weight, first_tangent, second_weight, second_tangent):
    gathered = gather(tokens, ROW, 32)
    token_count = gathered.shape[0]
    width = first_weight.shape[1]
    joined = jnp.concatenate([first_weight, first_tangent], axis=1)
    summed = scatter_sum_col(dot(gathered, joined, 1, 0))
    own_activation, derivative, own_tangent = activate(summed[:, :width], summed[:, width:])
    acts = gather_col(jnp.concatenate([own_activation, own_tangent], axis=1))
    activation, tangent_act = acts[:, :width], acts[:, width:]
    partial_out = dot(tangent_act, second_weight, 1, 0) + dot(activation, second_tangent, 1, 0)
    tangent_out = gather(scatter_sum(partial_out, ROW, 32).astype(bf16), ROW, 32)
    grad_act = scatter_sum_col(dot(tangent_out, second_weight, 1, 1))
    grad_pre = gather_col((grad_act * derivative).astype(bf16))
    scaling = 1.0 / math.sqrt(token_count)
    first_curvature = (dot(gathered, grad_pre, 0, 0) * scaling).astype(bf16)
    second_curvature = (dot(activation, tangent_out, 0, 0) * scaling).astype(bf16)
    return (first_curvature, second_curvature)


def solution(mesh):
    fine = Mesh(mesh.devices.reshape(4, 4, 2, 4, 4), ("z_lo", "y", "core", "x", "z_hi"))
    row, col = ROW, ("x", "z_hi")
    in_specs = (P(row, col), P(col, row), P(col, row), P(row, col), P(row, col))
    out_specs = (P(col, row), P(row, col))
    return jax.shard_map(shards, mesh=fine, in_specs=in_specs, out_specs=out_specs, check_vma=False)
```

```python
import math

import jax
import jax.numpy as jnp
from jax import lax
from jax.sharding import Mesh, PartitionSpec as P

sqrt_two_pi = 0.7978845608028654
cubic_coef = 0.044715

ROW = ("z_lo", "y", "core")
f32, bf16 = jnp.float32, jnp.bfloat16


def dot(left_side, right_side, left_dim, right_dim):
    return lax.dot_general(
        left_side, right_side, (((left_dim,), (right_dim,)), ((), ())), preferred_element_type=f32
    )


def swap(blocks, axes):
    return lax.all_to_all(blocks, axes, 0, 0, tiled=True)


def scatter_sum(partial, axes, count):
    arrived = swap(partial.astype(bf16), axes)
    return jnp.sum(arrived.reshape(count, -1, arrived.shape[1]).astype(f32), axis=0)


def gather(block, axes, count):
    return swap(jnp.broadcast_to(block[None], (count,) + block.shape).reshape(-1, block.shape[1]), axes)


def exchange_sum(partial, axes, count):
    arrived = gather(partial.astype(bf16), axes, count)
    return jnp.sum(arrived.reshape((count,) + partial.shape).astype(f32), axis=0)


def activate(hidden_pre, tangent_pre):
    inner_arg = sqrt_two_pi * (hidden_pre + cubic_coef * hidden_pre * hidden_pre * hidden_pre)
    hyper_tan = jnp.tanh(inner_arg)
    activation = (0.5 * hidden_pre * (1.0 + hyper_tan)).astype(bf16)
    derivative = 0.5 * (1.0 + hyper_tan) + 0.5 * hidden_pre * (
        1.0 - hyper_tan * hyper_tan
    ) * sqrt_two_pi * (1.0 + 3.0 * cubic_coef * hidden_pre * hidden_pre)
    tangent_act = (derivative * tangent_pre).astype(bf16)
    return (activation, derivative, tangent_act)


def shards(tokens, first_weight, first_tangent, second_weight, second_tangent):
    gathered = gather(tokens, ROW, 32)
    token_count = gathered.shape[0]
    width = first_weight.shape[1]
    joined = jnp.concatenate([first_weight, first_tangent], axis=1)
    summed = exchange_sum(scatter_sum(dot(gathered, joined, 1, 0), "x", 4), "z_hi", 4)
    own_activation, derivative, own_tangent = activate(summed[:, :width], summed[:, width:])
    acts = gather(jnp.concatenate([own_activation, own_tangent], axis=1), "x", 4)
    activation, tangent_act = acts[:, :width], acts[:, width:]
    partial_out = dot(tangent_act, second_weight, 1, 0) + dot(activation, second_tangent, 1, 0)
    out_share = exchange_sum(scatter_sum(partial_out, ("y", "core"), 8), "z_lo", 4).astype(bf16)
    tangent_out = gather(out_share, ("y", "core"), 8)
    grad_act = exchange_sum(scatter_sum(dot(tangent_out, second_weight, 1, 1), "x", 4), "z_hi", 4)
    grad_pre = gather((grad_act * derivative).astype(bf16), "x", 4)
    scaling = 1.0 / math.sqrt(token_count)
    first_curvature = (dot(gathered, grad_pre, 0, 0) * scaling).astype(bf16)
    second_curvature = (dot(activation, tangent_out, 0, 0) * scaling).astype(bf16)
    return (first_curvature, second_curvature)


def solution(mesh):
    fine = Mesh(mesh.devices.reshape(4, 4, 2, 4, 4), ("z_lo", "y", "core", "x", "z_hi"))
    row, col = ROW, ("x", "z_hi")
    in_specs = (P(row, col), P(col, row), P(col, row), P(row, col), P(row, col))
    out_specs = (P(col, row), P(row, col))
    return jax.shard_map(shards, mesh=fine, in_specs=in_specs, out_specs=out_specs, check_vma=False)
```

```python
import math

import jax
import jax.numpy as jnp
from jax import lax
from jax.sharding import Mesh, PartitionSpec as P

sqrt_two_pi = 0.7978845608028654
cubic_coef = 0.044715

ROW = ("z_lo", "y", "core")
f32, bf16 = jnp.float32, jnp.bfloat16


def dot(left_side, right_side, left_dim, right_dim):
    return lax.dot_general(
        left_side, right_side, (((left_dim,), (right_dim,)), ((), ())), preferred_element_type=f32
    )


def swap(blocks, axes):
    return lax.all_to_all(blocks, axes, 0, 0, tiled=True)


def scatter_sum(partial, axes, count):
    arrived = swap(partial.astype(bf16), axes)
    return jnp.sum(arrived.reshape(count, -1, arrived.shape[1]).astype(f32), axis=0)


def gather(block, axes, count):
    return swap(jnp.broadcast_to(block[None], (count,) + block.shape).reshape(-1, block.shape[1]), axes)


def exchange_sum(partial, axes, count):
    arrived = gather(partial.astype(bf16), axes, count)
    return jnp.sum(arrived.reshape((count,) + partial.shape).astype(f32), axis=0)


def activate(hidden_pre, tangent_pre):
    inner_arg = sqrt_two_pi * (hidden_pre + cubic_coef * hidden_pre * hidden_pre * hidden_pre)
    hyper_tan = jnp.tanh(inner_arg)
    activation = (0.5 * hidden_pre * (1.0 + hyper_tan)).astype(bf16)
    derivative = 0.5 * (1.0 + hyper_tan) + 0.5 * hidden_pre * (
        1.0 - hyper_tan * hyper_tan
    ) * sqrt_two_pi * (1.0 + 3.0 * cubic_coef * hidden_pre * hidden_pre)
    tangent_act = (derivative * tangent_pre).astype(bf16)
    return (activation, derivative, tangent_act)


def from_ahead(block, shift):
    return lax.ppermute(block, "x", [((i + shift) % 4, i) for i in range(4)])


def shards(tokens, first_weight, first_tangent, second_weight, second_tangent):
    together = lax.optimization_barrier
    gathered = gather(tokens, ROW, 32)
    weight_1, weight_3 = from_ahead(second_weight, 1), from_ahead(second_weight, 3)
    gathered, weight_1, weight_3 = together((gathered, weight_1, weight_3))
    token_count = gathered.shape[0]
    width = first_weight.shape[1]
    joined = jnp.concatenate([first_weight, first_tangent], axis=1)
    summed_x = scatter_sum(dot(gathered, joined, 1, 0), "x", 4).astype(bf16)
    summed_x, second_weight, second_tangent = together((summed_x, second_weight, second_tangent))

    weight_2 = from_ahead(second_weight, 2)
    tangent_1, tangent_3 = from_ahead(second_tangent, 1), from_ahead(second_tangent, 3)
    summed = scatter_sum(summed_x, "z_hi", 4)
    summed, weight_2, tangent_1, tangent_3, second_tangent = together(
        (summed, weight_2, tangent_1, tangent_3, second_tangent)
    )

    tangent_2 = from_ahead(second_tangent, 2)
    own_activation, derivative, own_tangent = activate(summed[:, :width], summed[:, width:])
    acts = gather(jnp.concatenate([own_activation, own_tangent], axis=1), "z_hi", 4)
    acts, tangent_2 = together((acts, tangent_2))

    weights = (second_weight, weight_1, weight_2, weight_3)
    tangents = (second_tangent, tangent_1, tangent_2, tangent_3)
    activation, tangent_act = acts[:, :width], acts[:, width:]
    partial_out = jnp.concatenate(
        [dot(tangent_act, w, 1, 0) + dot(activation, t, 1, 0) for w, t in zip(weights, tangents)], axis=0
    ).astype(bf16)
    partial_out, activation = together((partial_out, activation))

    all_acts = (activation,) + tuple(from_ahead(activation, shift) for shift in (1, 2, 3))
    share = scatter_sum(partial_out, ("y", "core"), 8)
    share, all_acts = together((share, all_acts))
    share = exchange_sum(share, "z_lo", 4).astype(bf16)
    tangent_out = gather(share, ("y", "core"), 8)
    outs = jnp.split(tangent_out, 4, axis=0)
    partial_grad = sum(dot(o, w, 1, 1) for o, w in zip(outs, weights)).astype(bf16)
    partial_grad, outs = together((partial_grad, outs))

    all_outs = (outs[0],) + tuple(from_ahead(outs[4 - shift], shift) for shift in (1, 2, 3))
    grad_act = scatter_sum(partial_grad, "z_hi", 4)
    grad_act, all_outs = together((grad_act, all_outs))
    grad_pre = gather(gather((grad_act * derivative).astype(bf16), "z_hi", 4), "x", 4)
    scaling = 1.0 / math.sqrt(token_count)
    first_curvature = (dot(gathered, grad_pre, 0, 0) * scaling).astype(bf16)
    second_curvature = (
        dot(jnp.concatenate(all_acts, axis=0), jnp.concatenate(all_outs, axis=0), 0, 0) * scaling
    ).astype(bf16)
    return (first_curvature, second_curvature)


def solution(mesh):
    fine = Mesh(mesh.devices.reshape(4, 4, 2, 4, 4), ("z_lo", "y", "core", "x", "z_hi"))
    row, col = ROW, ("x", "z_hi")
    in_specs = (P(row, col), P(col, row), P(col, row), P(row, col), P(row, col))
    out_specs = (P(col, row), P(row, col))
    return jax.shard_map(shards, mesh=fine, in_specs=in_specs, out_specs=out_specs, check_vma=False)
```

```python
import math

import jax
import jax.numpy as jnp
from jax import lax
from jax.experimental import pallas as pl
from jax.experimental.pallas import tpu as pltpu
from jax.sharding import Mesh, PartitionSpec as P

sqrt_two_pi = 0.7978845608028654
cubic_coef = 0.044715

ROW = ("z_lo", "y", "core")
f32, bf16 = jnp.float32, jnp.bfloat16


def dot(left_side, right_side, left_dim, right_dim):
    return lax.dot_general(
        left_side, right_side, (((left_dim,), (right_dim,)), ((), ())), preferred_element_type=f32
    )


def swap(blocks, axes):
    return lax.all_to_all(blocks, axes, 0, 0, tiled=True)


def scatter_sum(partial, axes, count):
    arrived = swap(partial.astype(bf16), axes)
    return jnp.sum(arrived.reshape(count, -1, arrived.shape[1]).astype(f32), axis=0)


def gather(block, axes, count):
    return swap(jnp.broadcast_to(block[None], (count,) + block.shape).reshape(-1, block.shape[1]), axes)


def exchange_sum(partial, axes, count):
    arrived = gather(partial.astype(bf16), axes, count)
    return jnp.sum(arrived.reshape((count,) + partial.shape).astype(f32), axis=0)


def activate(hidden_pre, tangent_pre):
    inner_arg = sqrt_two_pi * (hidden_pre + cubic_coef * hidden_pre * hidden_pre * hidden_pre)
    hyper_tan = jnp.tanh(inner_arg)
    activation = (0.5 * hidden_pre * (1.0 + hyper_tan)).astype(bf16)
    derivative = 0.5 * (1.0 + hyper_tan) + 0.5 * hidden_pre * (
        1.0 - hyper_tan * hyper_tan
    ) * sqrt_two_pi * (1.0 + 3.0 * cubic_coef * hidden_pre * hidden_pre)
    tangent_act = (derivative * tangent_pre).astype(bf16)
    return (activation, derivative, tangent_act)


def mm(left_side, right_side, left_dim, right_dim):
    return lax.dot_general(
        left_side, right_side, (((left_dim,), (right_dim,)), ((), ())), preferred_element_type=f32
    )


def out_kernel(acts_ref, tangents_ref, rest_ref, out_ref, copy_ref):
    head = tangents_ref.shape[1]
    width = acts_ref.shape[1] // 2
    activation, tangent_act = acts_ref[:, :width], acts_ref[:, width:]
    copy_ref[...] = acts_ref[...]
    for block in range(4):
        total = mm(tangent_act, rest_ref[block, :width], 1, 0)
        total += mm(activation[:, :head], tangents_ref[block], 1, 0)
        total += mm(activation[:, head:], rest_ref[block, width:], 1, 0)
        out_ref[block] = total.astype(bf16)


def grad_kernel(out_ref, rest_ref, grad_ref):
    width = grad_ref.shape[1]
    total = mm(out_ref[0], rest_ref[0, :width], 1, 1)
    for block in range(1, 4):
        total += mm(out_ref[block], rest_ref[block, :width], 1, 1)
    grad_ref[...] = total.astype(bf16)


PARAMS = pltpu.CompilerParams(vmem_limit_bytes=32 * 1024 * 1024)


def shards(tokens, first_weight, first_tangent, second_weight, second_tangent):
    together = lax.optimization_barrier
    width, features = second_weight.shape
    head = width // 4 * 3
    tangents = lax.all_gather(second_tangent[:head], "x")
    gathered = gather(tokens, ROW, 32)
    token_count = gathered.shape[0]
    joined = jnp.concatenate([first_weight, first_tangent], axis=1)
    summed_x = scatter_sum(dot(gathered, joined, 1, 0), "x", 4).astype(bf16)
    rest = jnp.concatenate([second_weight, second_tangent[head:]], axis=0)
    summed_x, rest = together((summed_x, rest))

    rest = lax.all_gather(rest, "x")
    summed = scatter_sum(summed_x, "z_hi", 4)
    own_activation, derivative, own_tangent = activate(summed[:, :width], summed[:, width:])
    acts = gather(jnp.concatenate([own_activation, own_tangent], axis=1), "z_hi", 4)

    share_rows = acts.shape[0]
    partial_out, acts = pl.pallas_call(
        out_kernel,
        out_shape=(
            jax.ShapeDtypeStruct((4, share_rows, features), bf16),
            jax.ShapeDtypeStruct(acts.shape, bf16),
        ),
        compiler_params=PARAMS,
    )(acts, tangents, rest)
    all_acts = lax.all_gather(acts, "x", tiled=True)
    share = scatter_sum(partial_out.reshape(-1, features), ("y", "core"), 8)
    share = exchange_sum(share, "z_lo", 4).astype(bf16)
    tangent_out = gather(share, ("y", "core"), 8)
    tangent_out, all_acts = together((tangent_out, all_acts))
    outs = tangent_out.reshape(4, share_rows, features)
    partial_grad = pl.pallas_call(
        grad_kernel, out_shape=jax.ShapeDtypeStruct((share_rows, width), bf16), compiler_params=PARAMS
    )(outs, rest)
    grad_act = scatter_sum(partial_grad, "z_hi", 4)
    grad_pre = gather((grad_act * derivative).astype(bf16), "z_hi", 4)
    grad_copies = jnp.broadcast_to(grad_pre[None], (4,) + grad_pre.shape)
    final = swap(jnp.concatenate([grad_copies, outs], axis=2), "x").reshape(token_count, -1)
    scaling = 1.0 / math.sqrt(token_count)
    first_curvature = (dot(gathered, final[:, :width], 0, 0) * scaling).astype(bf16)
    second_curvature = (dot(all_acts[:, :width], final[:, width:], 0, 0) * scaling).astype(bf16)
    return (first_curvature, second_curvature)


def solution(mesh):
    fine = Mesh(mesh.devices.reshape(4, 4, 2, 4, 4), ("z_lo", "y", "core", "x", "z_hi"))
    row, col = ROW, ("x", "z_hi")
    in_specs = (P(row, col), P(col, row), P(col, row), P(row, col), P(row, col))
    out_specs = (P(col, row), P(row, col))
    return jax.shard_map(shards, mesh=fine, in_specs=in_specs, out_specs=out_specs, check_vma=False)
```

```python
import math

import jax
import jax.numpy as jnp
from jax import lax
from jax.sharding import Mesh, PartitionSpec as P

sqrt_two_pi = 0.7978845608028654
cubic_coef = 0.044715

ROW = ("z_lo", "y", "core")
f32, bf16 = jnp.float32, jnp.bfloat16


def dot(left_side, right_side, left_dim, right_dim):
    return lax.dot_general(
        left_side, right_side, (((left_dim,), (right_dim,)), ((), ())), preferred_element_type=f32
    )


def swap(blocks, axes):
    return lax.all_to_all(blocks, axes, 0, 0, tiled=True)


def scatter_sum(partial, axes, count):
    arrived = swap(partial.astype(bf16), axes)
    return jnp.sum(arrived.reshape(count, -1, arrived.shape[1]).astype(f32), axis=0)


def gather(block, axes, count):
    return swap(jnp.broadcast_to(block[None], (count,) + block.shape).reshape(-1, block.shape[1]), axes)


def exchange_sum(partial, axes, count):
    arrived = gather(partial.astype(bf16), axes, count)
    return jnp.sum(arrived.reshape((count,) + partial.shape).astype(f32), axis=0)


def scatter_sum_col(partial):
    return scatter_sum(scatter_sum(partial, "x", 4), "z_hi", 4)


def gather_col(block):
    return gather(gather(block, "z_hi", 4), "x", 4)


def activate(hidden_pre, tangent_pre):
    inner_arg = sqrt_two_pi * (hidden_pre + cubic_coef * hidden_pre * hidden_pre * hidden_pre)
    hyper_tan = jnp.tanh(inner_arg)
    activation = (0.5 * hidden_pre * (1.0 + hyper_tan)).astype(bf16)
    derivative = 0.5 * (1.0 + hyper_tan) + 0.5 * hidden_pre * (
        1.0 - hyper_tan * hyper_tan
    ) * sqrt_two_pi * (1.0 + 3.0 * cubic_coef * hidden_pre * hidden_pre)
    tangent_act = (derivative * tangent_pre).astype(bf16)
    return (activation, derivative, tangent_act)


def shards(tokens, first_weight, first_tangent, second_weight, second_tangent):
    gathered = gather(tokens, ROW, 32)
    token_count = gathered.shape[0]
    width = first_weight.shape[1]
    joined = jnp.concatenate([first_weight, first_tangent], axis=1)
    summed = scatter_sum_col(dot(gathered, joined, 1, 0))
    own_activation, derivative, own_tangent = activate(summed[:, :width], summed[:, width:])
    acts = gather_col(jnp.concatenate([own_activation, own_tangent], axis=1))
    activation, tangent_act = acts[:, :width], acts[:, width:]
    partial_out = dot(tangent_act, second_weight, 1, 0) + dot(activation, second_tangent, 1, 0)
    out_share = exchange_sum(scatter_sum(partial_out, ("y", "core"), 8), "z_lo", 4).astype(bf16)
    tangent_out = gather(out_share, ("y", "core"), 8)
    grad_act = scatter_sum_col(dot(tangent_out, second_weight, 1, 1))
    grad_pre = gather_col((grad_act * derivative).astype(bf16))
    scaling = 1.0 / math.sqrt(token_count)
    first_curvature = (dot(gathered, grad_pre, 0, 0) * scaling).astype(bf16)
    second_curvature = (dot(activation, tangent_out, 0, 0) * scaling).astype(bf16)
    return (first_curvature, second_curvature)


def solution(mesh):
    fine = Mesh(mesh.devices.reshape(4, 4, 2, 4, 4), ("z_lo", "y", "core", "x", "z_hi"))
    row, col = ROW, ("x", "z_hi")
    in_specs = (P(row, col), P(col, row), P(col, row), P(row, col), P(row, col))
    out_specs = (P(col, row), P(row, col))
    return jax.shard_map(shards, mesh=fine, in_specs=in_specs, out_specs=out_specs, check_vma=False)
```

```python
import math

import jax
import jax.numpy as jnp
from jax import lax
from jax.experimental import pallas as pl
from jax.experimental.pallas import tpu as pltpu
from jax.sharding import Mesh, PartitionSpec as P

sqrt_two_pi = 0.7978845608028654
cubic_coef = 0.044715

ROW = ("z_lo", "y", "core")
f32, bf16 = jnp.float32, jnp.bfloat16


def dot(left_side, right_side, left_dim, right_dim):
    return lax.dot_general(
        left_side, right_side, (((left_dim,), (right_dim,)), ((), ())), preferred_element_type=f32
    )


def swap(blocks, axes):
    return lax.all_to_all(blocks, axes, 0, 0, tiled=True)


def scatter_sum(partial, axes, count):
    arrived = swap(partial.astype(bf16), axes)
    return jnp.sum(arrived.reshape(count, -1, arrived.shape[1]).astype(f32), axis=0)


def gather(block, axes, count):
    return swap(jnp.broadcast_to(block[None], (count,) + block.shape).reshape(-1, block.shape[1]), axes)


def exchange_sum(partial, axes, count):
    arrived = gather(partial.astype(bf16), axes, count)
    return jnp.sum(arrived.reshape((count,) + partial.shape).astype(f32), axis=0)


def scatter_sum_col(partial):
    return scatter_sum(scatter_sum(partial, "x", 4), "z_hi", 4)


def gather_col(block):
    return gather(gather(block, "z_hi", 4), "x", 4)


def activate(hidden_pre, tangent_pre):
    inner_arg = sqrt_two_pi * (hidden_pre + cubic_coef * hidden_pre * hidden_pre * hidden_pre)
    hyper_tan = jnp.tanh(inner_arg)
    activation = (0.5 * hidden_pre * (1.0 + hyper_tan)).astype(bf16)
    derivative = 0.5 * (1.0 + hyper_tan) + 0.5 * hidden_pre * (
        1.0 - hyper_tan * hyper_tan
    ) * sqrt_two_pi * (1.0 + 3.0 * cubic_coef * hidden_pre * hidden_pre)
    tangent_act = (derivative * tangent_pre).astype(bf16)
    return (activation, derivative, tangent_act)


def out_kernel(acts_ref, weight_ref, tangent_ref, out_ref):
    width = weight_ref.shape[0]
    total = dot(acts_ref[:, width:], weight_ref[...], 1, 0)
    out_ref[...] = (total + dot(acts_ref[:, :width], tangent_ref[...], 1, 0)).astype(bf16)


def call(kernel, *shape, **rest):
    params = pltpu.CompilerParams(vmem_limit_bytes=16 * 1024 * 1024)
    return pl.pallas_call(kernel, out_shape=jax.ShapeDtypeStruct(shape, bf16), compiler_params=params, **rest)


def shards(tokens, first_weight, first_tangent, second_weight, second_tangent):
    gathered = gather(gather(tokens, ("y", "core"), 8), "z_lo", 4)
    token_count = gathered.shape[0]
    width = first_weight.shape[1]
    joined = jnp.concatenate([first_weight, first_tangent], axis=1)
    summed = scatter_sum_col(dot(gathered, joined, 1, 0))
    own_activation, derivative, own_tangent = activate(summed[:, :width], summed[:, width:])
    acts = gather_col(jnp.concatenate([own_activation, own_tangent], axis=1))
    activation = acts[:, :width]
    partial_out = call(out_kernel, token_count, second_weight.shape[1])(acts, second_weight, second_tangent)
    out_share = exchange_sum(scatter_sum(partial_out, ("y", "core"), 8), "z_lo", 4).astype(bf16)
    tangent_out = gather(out_share, ("y", "core"), 8)
    grad_act = scatter_sum_col(dot(tangent_out, second_weight, 1, 1))
    grad_pre = gather_col((grad_act * derivative).astype(bf16))
    scaling = 1.0 / math.sqrt(token_count)
    first_curvature = (dot(gathered, grad_pre, 0, 0) * scaling).astype(bf16)
    second_curvature = (dot(activation, tangent_out, 0, 0) * scaling).astype(bf16)
    return (first_curvature, second_curvature)


def solution(mesh):
    fine = Mesh(mesh.devices.reshape(4, 4, 2, 4, 4), ("z_lo", "y", "core", "x", "z_hi"))
    row, col = ROW, ("x", "z_hi")
    in_specs = (P(row, col), P(col, row), P(col, row), P(row, col), P(row, col))
    out_specs = (P(col, row), P(row, col))
    return jax.shard_map(shards, mesh=fine, in_specs=in_specs, out_specs=out_specs, check_vma=False)
```

```python
import functools
import math

import jax
import jax.numpy as jnp
from jax import lax
from jax.experimental import pallas as pl
from jax.experimental.pallas import tpu as pltpu
from jax.sharding import Mesh, PartitionSpec as P

sqrt_two_pi = 0.7978845608028654
cubic_coef = 0.044715

ROW = ("z_lo", "y", "core")
f32, bf16 = jnp.float32, jnp.bfloat16


def dot(left_side, right_side, left_dim, right_dim):
    return lax.dot_general(
        left_side, right_side, (((left_dim,), (right_dim,)), ((), ())), preferred_element_type=f32
    )


def swap(blocks, axes):
    return lax.all_to_all(blocks, axes, 0, 0, tiled=True)


def scatter_sum(partial, axes, count):
    arrived = swap(partial.astype(bf16), axes)
    return jnp.sum(arrived.reshape(count, -1, arrived.shape[1]).astype(f32), axis=0)


def gather(block, axes, count):
    return swap(jnp.broadcast_to(block[None], (count,) + block.shape).reshape(-1, block.shape[1]), axes)


def exchange_sum(partial, axes, count):
    arrived = gather(partial.astype(bf16), axes, count)
    return jnp.sum(arrived.reshape((count,) + partial.shape).astype(f32), axis=0)


def scatter_sum_col(partial):
    return scatter_sum(scatter_sum(partial, "x", 4), "z_hi", 4)


def gather_col(block):
    return gather(gather(block, "z_hi", 4), "x", 4)


def activate(hidden_pre, tangent_pre):
    inner_arg = sqrt_two_pi * (hidden_pre + cubic_coef * hidden_pre * hidden_pre * hidden_pre)
    hyper_tan = jnp.tanh(inner_arg)
    activation = (0.5 * hidden_pre * (1.0 + hyper_tan)).astype(bf16)
    derivative = 0.5 * (1.0 + hyper_tan) + 0.5 * hidden_pre * (
        1.0 - hyper_tan * hyper_tan
    ) * sqrt_two_pi * (1.0 + 3.0 * cubic_coef * hidden_pre * hidden_pre)
    tangent_act = (derivative * tangent_pre).astype(bf16)
    return (activation, derivative, tangent_act)


def last_kernel(scaling, tokens_ref, grad_ref, acts_ref, outs_ref, first_ref, second_ref):
    width = second_ref.shape[0]
    second_ref[...] = (dot(acts_ref[:, :width], outs_ref[...], 0, 0) * scaling).astype(bf16)
    first_ref[...] = (dot(tokens_ref[...], grad_ref[...], 0, 0) * scaling).astype(bf16)


def out_kernel(acts_ref, weight_ref, tangent_ref, out_ref):
    width = weight_ref.shape[0]
    total = dot(acts_ref[:, width:], weight_ref[...], 1, 0)
    out_ref[...] = (total + dot(acts_ref[:, :width], tangent_ref[...], 1, 0)).astype(bf16)


def call(kernel, *shape, **rest):
    params = pltpu.CompilerParams(vmem_limit_bytes=16 * 1024 * 1024)
    return pl.pallas_call(kernel, out_shape=jax.ShapeDtypeStruct(shape, bf16), compiler_params=params, **rest)


def shards(tokens, first_weight, first_tangent, second_weight, second_tangent):
    gathered = gather(gather(tokens, ("y", "core"), 8), "z_lo", 4)
    token_count = gathered.shape[0]
    width = first_weight.shape[1]
    joined = jnp.concatenate([first_weight, first_tangent], axis=1)
    summed = scatter_sum_col(dot(gathered, joined, 1, 0))
    own_activation, derivative, own_tangent = activate(summed[:, :width], summed[:, width:])
    acts = gather_col(jnp.concatenate([own_activation, own_tangent], axis=1))
    partial_out = call(out_kernel, token_count, second_weight.shape[1])(acts, second_weight, second_tangent)
    out_share = exchange_sum(scatter_sum(partial_out, ("y", "core"), 8), "z_lo", 4).astype(bf16)
    tangent_out = gather(out_share, ("y", "core"), 8)
    grad_act = scatter_sum_col(dot(tangent_out, second_weight, 1, 1))
    grad_pre = gather_col((grad_act * derivative).astype(bf16))
    scaling = 1.0 / math.sqrt(token_count)
    features = gathered.shape[1]
    first_shape = jax.ShapeDtypeStruct((features, width), bf16)
    second_shape = jax.ShapeDtypeStruct((width, features), bf16)
    return pl.pallas_call(
        functools.partial(last_kernel, scaling),
        out_shape=(first_shape, second_shape),
        compiler_params=pltpu.CompilerParams(vmem_limit_bytes=16 * 1024 * 1024),
    )(gathered, grad_pre, acts, tangent_out)


def solution(mesh):
    fine = Mesh(mesh.devices.reshape(4, 4, 2, 4, 4), ("z_lo", "y", "core", "x", "z_hi"))
    row, col = ROW, ("x", "z_hi")
    in_specs = (P(row, col), P(col, row), P(col, row), P(row, col), P(row, col))
    out_specs = (P(col, row), P(row, col))
    return jax.shard_map(shards, mesh=fine, in_specs=in_specs, out_specs=out_specs, check_vma=False)
```

```python
import functools
import math

import jax
import jax.numpy as jnp
from jax import lax
from jax.experimental import pallas as pl
from jax.experimental.pallas import tpu as pltpu
from jax.sharding import Mesh, PartitionSpec as P

sqrt_two_pi = 0.7978845608028654
cubic_coef = 0.044715

ROW = ("z_lo", "y", "core")
f32, bf16 = jnp.float32, jnp.bfloat16


def dot(left_side, right_side, left_dim, right_dim):
    return lax.dot_general(
        left_side, right_side, (((left_dim,), (right_dim,)), ((), ())), preferred_element_type=f32
    )


def swap(blocks, axes):
    return lax.all_to_all(blocks, axes, 0, 0, tiled=True)


def scatter_sum(partial, axes, count):
    arrived = swap(partial.astype(bf16), axes)
    return jnp.sum(arrived.reshape(count, -1, arrived.shape[1]).astype(f32), axis=0)


def gather(block, axes, count):
    return swap(jnp.broadcast_to(block[None], (count,) + block.shape).reshape(-1, block.shape[1]), axes)


def exchange_sum(partial, axes, count):
    arrived = gather(partial.astype(bf16), axes, count)
    return jnp.sum(arrived.reshape((count,) + partial.shape).astype(f32), axis=0)


def scatter_sum_col(partial):
    return scatter_sum(scatter_sum(partial, "x", 4), "z_hi", 4)


def gather_col(block):
    return gather(gather(block, "z_hi", 4), "x", 4)


def activate(hidden_pre, tangent_pre):
    inner_arg = sqrt_two_pi * (hidden_pre + cubic_coef * hidden_pre * hidden_pre * hidden_pre)
    hyper_tan = jnp.tanh(inner_arg)
    activation = (0.5 * hidden_pre * (1.0 + hyper_tan)).astype(bf16)
    derivative = 0.5 * (1.0 + hyper_tan) + 0.5 * hidden_pre * (
        1.0 - hyper_tan * hyper_tan
    ) * sqrt_two_pi * (1.0 + 3.0 * cubic_coef * hidden_pre * hidden_pre)
    tangent_act = (derivative * tangent_pre).astype(bf16)
    return (activation, derivative, tangent_act)


def last_kernel(scaling, tokens_ref, grad_ref, acts_ref, outs_ref, first_ref, second_ref):
    width = second_ref.shape[0]
    second_ref[...] = (dot(acts_ref[:, :width], outs_ref[...], 0, 0) * scaling).astype(bf16)
    first_ref[...] = (dot(tokens_ref[...], grad_ref[...], 0, 0) * scaling).astype(bf16)


def out_kernel(acts_ref, weight_ref, tangent_ref, out_ref):
    width = weight_ref.shape[0]
    total = dot(acts_ref[:, width:], weight_ref[...], 1, 0)
    out_ref[...] = (total + dot(acts_ref[:, :width], tangent_ref[...], 1, 0)).astype(bf16)


def call(kernel, *shape, **rest):
    params = pltpu.CompilerParams(vmem_limit_bytes=16 * 1024 * 1024)
    return pl.pallas_call(kernel, out_shape=jax.ShapeDtypeStruct(shape, bf16), compiler_params=params, **rest)


def shards(tokens, first_weight, first_tangent, second_weight, second_tangent):
    gathered = gather(gather(tokens, ("y", "core"), 8), "z_lo", 4)
    token_count = gathered.shape[0]
    width = first_weight.shape[1]
    joined = jnp.concatenate([first_weight, first_tangent], axis=1)
    summed = scatter_sum_col(dot(gathered, joined, 1, 0))
    own_activation, derivative, own_tangent = activate(summed[:, :width], summed[:, width:])
    own_acts = jnp.concatenate([own_activation, own_tangent], axis=1)
    acts = gather(lax.all_gather(own_acts, "z_hi", tiled=True), "x", 4)
    partial_out = call(out_kernel, token_count, second_weight.shape[1])(acts, second_weight, second_tangent)
    out_share = exchange_sum(scatter_sum(partial_out, ("y", "core"), 8), "z_lo", 4).astype(bf16)
    tangent_out = gather(out_share, ("y", "core"), 8)
    grad_act = scatter_sum_col(dot(tangent_out, second_weight, 1, 1))
    grad_pre = gather_col((grad_act * derivative).astype(bf16))
    scaling = 1.0 / math.sqrt(token_count)
    features = gathered.shape[1]
    first_shape = jax.ShapeDtypeStruct((features, width), bf16)
    second_shape = jax.ShapeDtypeStruct((width, features), bf16)
    return pl.pallas_call(
        functools.partial(last_kernel, scaling),
        out_shape=(first_shape, second_shape),
        compiler_params=pltpu.CompilerParams(vmem_limit_bytes=16 * 1024 * 1024),
    )(gathered, grad_pre, acts, tangent_out)


def solution(mesh):
    fine = Mesh(mesh.devices.reshape(4, 4, 2, 4, 4), ("z_lo", "y", "core", "x", "z_hi"))
    row, col = ROW, ("x", "z_hi")
    in_specs = (P(row, col), P(col, row), P(col, row), P(row, col), P(row, col))
    out_specs = (P(col, row), P(row, col))
    return jax.shard_map(shards, mesh=fine, in_specs=in_specs, out_specs=out_specs, check_vma=False)
```

```python
import functools
import math

import jax
import jax.numpy as jnp
from jax import lax
from jax.experimental import pallas as pl
from jax.experimental.pallas import tpu as pltpu
from jax.sharding import Mesh, PartitionSpec as P

sqrt_two_pi = 0.7978845608028654
cubic_coef = 0.044715

ROW = ("z_lo", "y", "core")
f32, bf16 = jnp.float32, jnp.bfloat16


def dot(left_side, right_side, left_dim, right_dim):
    return lax.dot_general(
        left_side, right_side, (((left_dim,), (right_dim,)), ((), ())), preferred_element_type=f32
    )


def swap(blocks, axes):
    return lax.all_to_all(blocks, axes, 0, 0, tiled=True)


def scatter_sum(partial, axes, count):
    arrived = swap(partial.astype(bf16), axes)
    return jnp.sum(arrived.reshape(count, -1, arrived.shape[1]).astype(f32), axis=0)


def gather(block, axes, count):
    return swap(jnp.broadcast_to(block[None], (count,) + block.shape).reshape(-1, block.shape[1]), axes)


def exchange_sum(partial, axes, count):
    arrived = gather(partial.astype(bf16), axes, count)
    return jnp.sum(arrived.reshape((count,) + partial.shape).astype(f32), axis=0)


def scatter_sum_col(partial):
    return scatter_sum(scatter_sum(partial, "x", 4), "z_hi", 4)


def gather_col(block):
    return gather(gather(block, "z_hi", 4), "x", 4)


def activate(hidden_pre, tangent_pre):
    inner_arg = sqrt_two_pi * (hidden_pre + cubic_coef * hidden_pre * hidden_pre * hidden_pre)
    hyper_tan = jnp.tanh(inner_arg)
    activation = (0.5 * hidden_pre * (1.0 + hyper_tan)).astype(bf16)
    derivative = 0.5 * (1.0 + hyper_tan) + 0.5 * hidden_pre * (
        1.0 - hyper_tan * hyper_tan
    ) * sqrt_two_pi * (1.0 + 3.0 * cubic_coef * hidden_pre * hidden_pre)
    tangent_act = (derivative * tangent_pre).astype(bf16)
    return (activation, derivative, tangent_act)


def last_kernel(scaling, tokens_ref, grad_ref, acts_ref, outs_ref, first_ref, second_ref, first, second, sems):
    width = second.shape[0]
    second[...] = (dot(acts_ref[:, :width], outs_ref[...], 0, 0) * scaling).astype(bf16)
    second_out = pltpu.make_async_copy(second, second_ref, sems.at[0])
    second_out.start()
    first[...] = (dot(tokens_ref[...], grad_ref[...], 0, 0) * scaling).astype(bf16)
    first_out = pltpu.make_async_copy(first, first_ref, sems.at[1])
    first_out.start()
    second_out.wait()
    first_out.wait()


def out_kernel(acts_ref, weight_ref, tangent_ref, out_ref):
    width = weight_ref.shape[0]
    total = dot(acts_ref[:, width:], weight_ref[...], 1, 0)
    out_ref[...] = (total + dot(acts_ref[:, :width], tangent_ref[...], 1, 0)).astype(bf16)


def call(kernel, *shape, **rest):
    params = pltpu.CompilerParams(vmem_limit_bytes=16 * 1024 * 1024)
    return pl.pallas_call(kernel, out_shape=jax.ShapeDtypeStruct(shape, bf16), compiler_params=params, **rest)


def shards(tokens, first_weight, first_tangent, second_weight, second_tangent):
    gathered = gather(gather(tokens, ("y", "core"), 8), "z_lo", 4)
    token_count = gathered.shape[0]
    width = first_weight.shape[1]
    joined = jnp.concatenate([first_weight, first_tangent], axis=1)
    summed = scatter_sum_col(dot(gathered, joined, 1, 0))
    own_activation, derivative, own_tangent = activate(summed[:, :width], summed[:, width:])
    own_acts = jnp.concatenate([own_activation, own_tangent], axis=1)
    acts = gather(lax.all_gather(own_acts, "z_hi", tiled=True), "x", 4)
    partial_out = call(out_kernel, token_count, second_weight.shape[1])(acts, second_weight, second_tangent)
    out_share = exchange_sum(scatter_sum(partial_out, ("y", "core"), 8), "z_lo", 4).astype(bf16)
    tangent_out = gather(out_share, ("y", "core"), 8)
    grad_act = scatter_sum_col(dot(tangent_out, second_weight, 1, 1))
    grad_pre = gather_col((grad_act * derivative).astype(bf16))
    scaling = 1.0 / math.sqrt(token_count)
    features = gathered.shape[1]
    first_shape = jax.ShapeDtypeStruct((features, width), bf16)
    second_shape = jax.ShapeDtypeStruct((width, features), bf16)
    return tuple(pl.pallas_call(
        functools.partial(last_kernel, scaling),
        out_shape=[first_shape, second_shape],
        out_specs=[pl.BlockSpec(memory_space=pl.ANY)] * 2,
        scratch_shapes=[
            pltpu.VMEM((features, width), bf16),
            pltpu.VMEM((width, features), bf16),
            pltpu.SemaphoreType.DMA((2,)),
        ],
        compiler_params=pltpu.CompilerParams(vmem_limit_bytes=16 * 1024 * 1024),
    )(gathered, grad_pre, acts, tangent_out))


def solution(mesh):
    fine = Mesh(mesh.devices.reshape(4, 4, 2, 4, 4), ("z_lo", "y", "core", "x", "z_hi"))
    row, col = ROW, ("x", "z_hi")
    in_specs = (P(row, col), P(col, row), P(col, row), P(row, col), P(row, col))
    out_specs = (P(col, row), P(row, col))
    return jax.shard_map(shards, mesh=fine, in_specs=in_specs, out_specs=out_specs, check_vma=False)
```
